32 devices in a mesh: box: 8 (over z, y), dir: 4 (over x, core).
Axes of the slice: x: 2, y: 2, z: 4, core: 2. Of those that a mesh axis runs over, the one named last changes fastest.
Arguments:
- pattern: float32 [512, 8, 4096], P('dir', None, 'box'), may hold values from -6 to 6
- child_coef: float32 [2, 4, 512], P(None, None, 'dir'), may hold values from -3 to 3
- child_mask: int32 [4, 4096], P(None, 'box'), may hold values 0 or 1
- interp_index: int32 [16, 2048], replicated, may hold values from 0 to 511, as said below
- interp_weight: float32 [16, 2048], replicated, may hold values from -1.25 to 1.25
- phase_angle: float32 [8, 2048], replicated, may hold values from -3.140625 to 3.140625
- parent_coef: float32 [2, 32, 2048], replicated, may hold values from -3 to 3
- parent_mask: int32 [32, 512], replicated, may hold values 0 or 1
Outputs:
- local_field: float32 [512, 8, 4096], P('dir', None, 'box')
The draws below stay inside these ranges and needn't reach their ends.
Inputs may be any that keep to these rules, and one draw needn't show every extreme that they name: `interp_index`: child directions form a grid of 16 polar by 32 azimuthal angles, numbered as (azimuth % 4) * 128 + polar * 8 + azimuth // 4; each parent direction reads the 16 child directions of a 4 by 4 block of neighbouring angles, the azimuth wrapping round.
All inputs are finite; a program needn't handle non-finite values. No bound on the sum of `child_mask` on one device may be relied on, other than what follows from the above.
Results may differ from the reference program's by a relative error of at most 0.000053.
Values sent between devices are 32-bit elements; how exact they have to be, the bound alone decides.
A program may use at most 192 MiB of HBM per device.

```python
import jax
import jax.numpy as jnp
from jax import lax

CHILD_DIRS = 512
PARENT_DIRS = 2048
CHILD_THETA = 16
RHS = 4
GROUP = 8
POINTS = 16
CHILD_REACH = 2
PARENT_REACH = 16
BOX_DEV = 512
BOXES = 4096
PAR_DEV = 64
PARENTS = 512
N_BOX = 8


def draw_interp_index(key, part):
    child_theta = CHILD_THETA
    child_phi = 2 * CHILD_THETA
    parent_phi = 2 * child_phi
    parent = jnp.arange(PARENT_DIRS, dtype=jnp.int32)
    theta_parent = parent // parent_phi
    phi_parent = parent % parent_phi
    key_theta, key_phi = jax.random.split(jax.random.fold_in(key, 7))
    jitter_theta = jax.random.randint(key_theta, (PARENT_DIRS,), -1, 2, dtype=jnp.int32)
    jitter_phi = jax.random.randint(key_phi, (PARENT_DIRS,), -1, 2, dtype=jnp.int32)
    theta_start = jnp.clip(theta_parent // 2 - 1 + jitter_theta, 0, child_theta - 4)
    phi_start = phi_parent // 2 - 1 + jitter_phi + child_phi
    point = jnp.arange(POINTS, dtype=jnp.int32)
    theta_child = theta_start[None, :] + (point // 4)[:, None]
    phi_child = (phi_start[None, :] + (point % 4)[:, None]) % child_phi
    index = phi_child % 4 * (CHILD_DIRS // 4) + theta_child * (child_phi // 4) + phi_child // 4
    return index.astype(jnp.int32)


def touch_ends(entries, rng, low, top_value):
    spot = [jax.random.randint(jax.random.fold_in(rng, axis), (), 0, length) for axis, length in enumerate(entries.shape)]
    longest = entries.shape.index(max(entries.shape))
    neighbour = spot[:longest] + [(spot[longest] + 1) % entries.shape[longest]] + spot[longest + 1:]
    return entries.at[tuple(spot)].set(low).at[tuple(neighbour)].set(top_value)


def block_levels(stream_key, extent, cuts, smallest, high):
    level, own = 1.0, jax.random.fold_in(stream_key, 6)
    for dim, blocks in cuts:
        heights = jnp.exp(jax.random.uniform(jax.random.fold_in(own, dim), (blocks,), jnp.float32, smallest / len(cuts), high / len(cuts)))
        level = level * jnp.repeat(heights, extent[dim] // blocks).reshape([-1 if axis == dim else 1 for axis in range(len(extent))])
    return level


def centred(rng, dims, scale, limit, cuts=(), kind=jnp.bfloat16):
    drawn = scale * jax.random.normal(rng, dims, jnp.float32)
    if cuts:
        drawn = drawn * block_levels(rng, dims, cuts, -0.22, 0.18)
    return jnp.clip(drawn, -limit, limit).astype(kind)


def setup_inputs(seed: int = 0) -> dict:
    seeds = jax.random.split(jax.random.key(seed), 9)
    pattern = centred(seeds[0], (CHILD_DIRS, 2 * RHS, BOXES), 1.0, 6.0, ((0, 4), (2, 8)), jnp.float32)
    child_coef = centred(seeds[1], (2, 2 * CHILD_REACH, CHILD_DIRS), 0.5, 3.0, ((2, 4),), jnp.float32)
    child_mask = touch_ends((jax.random.randint(seeds[2], (2 * CHILD_REACH, BOXES), 0, 4) < 3).astype(jnp.int32), jax.random.fold_in(seeds[2], 1), 0, 1)
    interp_index = draw_interp_index(jax.random.fold_in(seeds[8], 71), 0)
    interp_weight = centred(seeds[4], (POINTS, PARENT_DIRS), 0.09, 1.25, (), jnp.float32)
    phase_angle = jnp.clip(jax.random.uniform(seeds[5], (GROUP, PARENT_DIRS), jnp.float32, -3.140625, 3.140625), -3.140625, 3.140625)
    parent_coef = centred(seeds[6], (2, 2 * PARENT_REACH, PARENT_DIRS), 0.2, 3.0, (), jnp.float32)
    parent_mask = touch_ends((jax.random.randint(seeds[7], (2 * PARENT_REACH, PARENTS), 0, 4) < 3).astype(jnp.int32), jax.random.fold_in(seeds[7], 1), 0, 1)
    return {"pattern": pattern, "child_coef": child_coef, "child_mask": child_mask, "interp_index": interp_index, "interp_weight": interp_weight, "phase_angle": phase_angle, "parent_coef": parent_coef, "parent_mask": parent_mask}


def interp_matrix(index, weight, first_row, row_count):
    rows = first_row + lax.iota(jnp.int32, row_count)
    matrix = jnp.zeros((row_count, index.shape[1]), jnp.float32)
    for point in range(index.shape[0]):
        matrix = matrix + jnp.where(rows[:, None] == index[point][None, :], weight[point][None, :], jnp.float32(0.0))
    return matrix


def translate_padded(padded, coef_real, coef_imag, mask, reach):
    count = padded.shape[2] - 2 * reach
    half = padded.shape[1] // 2
    offsets = list(range(-reach, 0)) + list(range(1, reach + 1))
    summed = jnp.zeros((padded.shape[0], padded.shape[1], count), jnp.float32)
    for position, offset in enumerate(offsets):
        source = padded[:, :, reach + offset:reach + offset + count]
        real_part = source[:, :half]
        imag_part = source[:, half:]
        scale_real = coef_real[position][:, None, None]
        scale_imag = coef_imag[position][:, None, None]
        weight = mask[position].astype(jnp.float32)[None, None, :]
        turned = jnp.concatenate([scale_real * real_part - scale_imag * imag_part, scale_real * imag_part + scale_imag * real_part], axis=1)
        summed = summed + weight * turned
    return summed


def aggregate(raw, cosine, sine_table):
    direction_count, component_count, box_count = raw.shape
    half = component_count // 2
    group = cosine.shape[1]
    cos_box = jnp.tile(cosine, (1, box_count // group))[:, None, :]
    sin_box = jnp.tile(sine_table, (1, box_count // group))[:, None, :]
    real_part = raw[:, :half]
    imag_part = raw[:, half:]
    turned = jnp.concatenate([cos_box * real_part - sin_box * imag_part, cos_box * imag_part + sin_box * real_part], axis=1)
    return turned.reshape(direction_count, component_count, box_count // group, group).sum(axis=3)


def disaggregate(local, cosine, sine_table):
    group = cosine.shape[1]
    expanded = jnp.repeat(local, group, axis=2)
    box_count = expanded.shape[2]
    half = expanded.shape[1] // 2
    cos_box = jnp.tile(cosine, (1, box_count // group))[:, None, :]
    sin_box = jnp.tile(sine_table, (1, box_count // group))[:, None, :]
    real_part = expanded[:, :half]
    imag_part = expanded[:, half:]
    return jnp.concatenate([cos_box * real_part + sin_box * imag_part, cos_box * imag_part - sin_box * real_part], axis=1)


def reference(pattern, child_coef, child_mask, interp_index, interp_weight, phase_angle, parent_coef, parent_mask):
    highest = lax.Precision.HIGHEST
    matrix = interp_matrix(interp_index, interp_weight, 0, CHILD_DIRS)
    cosine = jnp.cos(phase_angle).T
    sine_table = jnp.sin(phase_angle).T
    blocks = jnp.arange(N_BOX, dtype=jnp.int32)

    def upward(block):
        piece = lax.dynamic_slice_in_dim(pattern, block * BOX_DEV, BOX_DEV, 2)
        raw = jnp.einsum("qp,qcb->pcb", matrix, piece, precision=highest)
        return aggregate(raw, cosine, sine_table)

    parent_blocks = lax.map(upward, blocks)
    parent_field = jnp.transpose(parent_blocks, (1, 2, 0, 3)).reshape(PARENT_DIRS, 2 * RHS, PARENTS)
    parent_padded = jnp.pad(parent_field, ((0, 0), (0, 0), (PARENT_REACH, PARENT_REACH)))
    parent_local = translate_padded(parent_padded, parent_coef[0], parent_coef[1], parent_mask, PARENT_REACH)
    child_padded = jnp.pad(pattern, ((0, 0), (0, 0), (CHILD_REACH, CHILD_REACH)))
    child_local = translate_padded(child_padded, child_coef[0], child_coef[1], child_mask, CHILD_REACH)

    def downward(block):
        local_piece = lax.dynamic_slice_in_dim(parent_local, block * PAR_DEV, PAR_DEV, 2)
        spread = disaggregate(local_piece, cosine, sine_table)
        return jnp.einsum("qp,pcb->qcb", matrix, spread, precision=highest)

    far_blocks = lax.map(downward, blocks)
    far_part = jnp.transpose(far_blocks, (1, 2, 0, 3)).reshape(CHILD_DIRS, 2 * RHS, BOXES)
    return child_local + far_part
```

```python
import functools

import jax
import jax.numpy as jnp
from jax import lax
from jax.experimental import pallas as pl
from jax.experimental.pallas import tpu as pltpu
from jax.sharding import PartitionSpec as P

F32, BF16 = jnp.float32, jnp.bfloat16
VMEM_LIMIT = 56 * 1024 * 1024


def split(x):
    hi = x.astype(BF16)
    return hi, (x - hi.astype(F32)).astype(BF16)


def turn(x):
    half = x.shape[1] // 2
    return jnp.concatenate([-x[:, half:], x[:, :half]], axis=1)


def nn(a, b):
    return lax.dot_general(a, b, (((1,), (0,)), ((), ())), preferred_element_type=F32)


def nt(a, b):
    return lax.dot_general(a, b, (((1,), (1,)), ((), ())), preferred_element_type=F32)


def build_weights(first, idx, wgt, cos, sin, whi, wlo):
    points, p = idx.shape
    group = cos.shape[0]
    q = whi.shape[0] // (2 * group)
    rows = first + lax.broadcasted_iota(jnp.int32, (q, p), 0)
    m = jnp.zeros((q, p), F32)
    for k in range(points):
        m = m + jnp.where(rows == idx[k : k + 1, :], wgt[k : k + 1, :], F32(0.0))
    for part, table in enumerate((cos, sin)):
        for g in range(group):
            hi, lo = split(m * table[g : g + 1, :])
            at = (part * group + g) * q
            whi[at : at + q, :] = hi
            wlo[at : at + q, :] = lo


def up_kernel(idx, wgt, cos, sin, pat, out, xhi, xlo, whi, wlo):
    q = pat.shape[2]
    group = cos.shape[0]
    s_count = pat.shape[0] // group
    rows = s_count * pat.shape[1]

    @pl.when(pl.program_id(0) == 0)
    def _():
        for g in range(group):
            x = pat[...].reshape(s_count, group, pat.shape[1], q)[:, g]
            for part, y in enumerate((x, turn(x))):
                hi, lo = split(y.reshape(rows, q))
                at = (part * group + g) * q
                xhi[:, at : at + q] = hi
                xlo[:, at : at + q] = lo

    first = lax.axis_index("dir") * q
    build_weights(first, idx[...], wgt[...], cos[...], sin[...], whi, wlo)
    total = nn(xhi[...], whi[...]) + nn(xhi[...], wlo[...]) + nn(xlo[...], whi[...])
    out[...] = total.reshape(s_count, pat.shape[1], -1)


def translate_kernel(field, coef, mask, out, *, reach):
    count = out.shape[0]
    offsets = list(range(-reach, 0)) + list(range(1, reach + 1))
    block = 4

    def step(i, _):
        s0 = i * block
        for lane in range(0, out.shape[2], 128):
            real = [jnp.zeros((out.shape[1], 128), F32) for _ in range(block)]
            imag = [jnp.zeros((out.shape[1], 128), F32) for _ in range(block)]
            for k, t in enumerate(offsets):
                cr = coef[0, k : k + 1, lane : lane + 128]
                ci = coef[1, k : k + 1, lane : lane + 128]
                for j in range(block):
                    f = field[s0 + j + reach + t, :, lane : lane + 128] * mask[k, s0 + j]
                    real[j] = real[j] + f * cr
                    imag[j] = imag[j] + f * ci
            for j in range(block):
                half = out.shape[1] // 2
                b = imag[j]
                out[s0 + j, :, lane : lane + 128] = real[j] + jnp.concatenate([-b[half:], b[:half]], axis=0)
        return 0

    lax.fori_loop(0, count // block, step, 0)


def down_kernel(idx, wgt, cos, sin, loc, child, out, acc, whi, wlo):
    group = cos.shape[0]
    s_count, comps, p = loc.shape
    q = out.shape[2]
    step = pl.program_id(0)
    first = lax.axis_index("dir") * q
    build_weights(first, idx[...], wgt[...], cos[...], sin[...], whi, wlo)
    x = loc[...]
    n = group * q
    total = None
    for part, y in enumerate((x, -turn(x))):
        hi, lo = split(y.reshape(s_count * comps, p))
        wh, wl = whi[part * n : (part + 1) * n, :], wlo[part * n : (part + 1) * n, :]
        for term in (nt(hi, wh), nt(hi, wl), nt(lo, wh)):
            total = term if total is None else total + term

    @pl.when(step == 0)
    def _():
        acc[...] = total

    @pl.when(step > 0)
    def _():
        acc[...] = acc[...] + total

    @pl.when(step == pl.num_programs(0) - 1)
    def _():
        for g in range(group):
            def put(s, _):
                at = pl.ds(pl.multiple_of(s * comps, comps), comps)
                out[s * group + g] = acc[at, g * q : (g + 1) * q] + child[s * group + g]
                return 0
            lax.fori_loop(0, s_count, put, 0)


def halo(block, width):
    count = lax.axis_size("box")
    forward = [(i, i + 1) for i in range(count - 1)]
    backward = [(b, a) for a, b in forward]
    low = lax.ppermute(block[-width:], "box", forward)
    high = lax.ppermute(block[:width], "box", backward)
    return jnp.concatenate([low, block, high], axis=0)


def body(pattern, child_coef, child_mask, interp_index, interp_weight, phase_angle, parent_coef, parent_mask):
    q, comps, boxes = pattern.shape
    p_all = interp_index.shape[1]
    group = phase_angle.shape[0]
    s_count = boxes // group
    dir_size = lax.axis_size("dir")
    p_own = p_all // dir_size
    dir_rank = lax.axis_index("dir")
    box_rank = lax.axis_index("box")
    cos, sin = jnp.cos(phase_angle), jnp.sin(phase_angle)
    pat = jnp.transpose(pattern, (2, 1, 0))
    chunk = 256
    col = lambda rows: pl.BlockSpec((rows, chunk), lambda i: (0, i))
    params = pltpu.CompilerParams(vmem_limit_bytes=VMEM_LIMIT)
    wsize = 2 * group * q
    rows = s_count * comps
    whole = lambda shape: pl.BlockSpec(shape, lambda i: (0,) * len(shape))
    field = pl.pallas_call(
        up_kernel,
        grid=(p_all // chunk,),
        out_shape=jax.ShapeDtypeStruct((s_count, comps, p_all), F32),
        in_specs=[col(interp_index.shape[0]), col(interp_index.shape[0]), col(group), col(group), whole(pat.shape)],
        out_specs=pl.BlockSpec((s_count, comps, chunk), lambda i: (0, 0, i)),
        scratch_shapes=[pltpu.VMEM((rows, wsize), BF16)] * 2 + [pltpu.VMEM((wsize, chunk), BF16)] * 2,
        compiler_params=params,
    )(interp_index, interp_weight, cos, sin, pat)
    field = lax.psum_scatter(field, "dir", scatter_dimension=2, tiled=True)

    def translate(x, coef, mask, reach):
        return pl.pallas_call(
            functools.partial(translate_kernel, reach=reach),
            out_shape=jax.ShapeDtypeStruct((x.shape[0] - 2 * reach,) + x.shape[1:], F32),
            in_specs=[
                pl.BlockSpec(memory_space=pltpu.VMEM),
                pl.BlockSpec(memory_space=pltpu.VMEM),
                pl.BlockSpec(memory_space=pltpu.SMEM),
            ],
            compiler_params=params,
        )(x, coef, mask.astype(F32))

    child_reach = child_coef.shape[1] // 2
    child = translate(halo(pat, child_reach), child_coef, child_mask, child_reach)
    reach = parent_coef.shape[1] // 2
    own_coef = lax.dynamic_slice_in_dim(parent_coef, dir_rank * p_own, p_own, 2)
    own_mask = lax.dynamic_slice_in_dim(parent_mask, box_rank * s_count, s_count, 1)
    local = translate(halo(field, reach), own_coef, own_mask, reach)
    local = lax.all_gather(local, "dir", axis=2, tiled=True)
    out = pl.pallas_call(
        down_kernel,
        grid=(p_all // chunk,),
        out_shape=jax.ShapeDtypeStruct((boxes, comps, q), F32),
        in_specs=[
            col(interp_index.shape[0]), col(interp_index.shape[0]), col(group), col(group),
            pl.BlockSpec((s_count, comps, chunk), lambda i: (0, 0, i)),
            whole(pat.shape),
        ],
        out_specs=whole(pat.shape),
        scratch_shapes=[pltpu.VMEM((rows, group * q), F32)] + [pltpu.VMEM((wsize, chunk), BF16)] * 2,
        compiler_params=params,
    )(interp_index, interp_weight, cos, sin, local, child)
    return jnp.transpose(out, (2, 1, 0))


def solution(mesh):
    placed = (P("dir", None, "box"), P(None, None, "dir"), P(None, "box"), P(), P(), P(), P(), P())
    return jax.shard_map(
        body, mesh=mesh, in_specs=placed, out_specs=P("dir", None, "box"), check_vma=False
    )
```

```python
import functools

import jax
import jax.numpy as jnp
from jax import lax
from jax.experimental import pallas as pl
from jax.experimental.pallas import tpu as pltpu
from jax.sharding import PartitionSpec as P

F32, BF16 = jnp.float32, jnp.bfloat16
VMEM_LIMIT = 60 * 1024 * 1024
MESH = pl.DeviceIdType.MESH


def split(x):
    hi = x.astype(BF16)
    return hi, (x - hi.astype(F32)).astype(BF16)


def turn(x):
    half = x.shape[1] // 2
    return jnp.concatenate([-x[:, half:], x[:, :half]], axis=1)


def nn(a, b):
    return lax.dot_general(a, b, (((1,), (0,)), ((), ())), preferred_element_type=F32)


def nt(a, b):
    return lax.dot_general(a, b, (((1,), (1,)), ((), ())), preferred_element_type=F32)


def translate(field, at, coef, mask, put, s0, count, reach, block=4):
    comps = field(0).shape[0]
    half = comps // 2
    offsets = list(range(-reach, 0)) + list(range(1, reach + 1))

    def step(i, _):
        s = s0 + i * block
        real = [jnp.zeros((comps, 128), F32) for _ in range(block)]
        imag = [jnp.zeros((comps, 128), F32) for _ in range(block)]
        for k, t in enumerate(offsets):
            cr, ci = coef(0, k), coef(1, k)
            for j in range(block):
                f = field(at + s + j + t) * mask(k, s + j)
                real[j] = real[j] + f * cr
                imag[j] = imag[j] + f * ci
        for j in range(block):
            b = imag[j]
            put(s + j, real[j] + jnp.concatenate([-b[half:], b[:half]], axis=0))
        return 0

    lax.fori_loop(0, count // block, step, 0)


def kernel(
    idx, wgt, cos, sin, child_coef, coef, child_mask, mask, pat,
    out,
    cbuf, xhi, xlo, whi, wlo, part, crecv, xsend, xrecv, field, gl, acc,
    local_sem, ch_send, ch_recv, core_send, core_recv, x_send, x_recv, halo_send, halo_recv,
    lx_send, lx_recv, lc_send, lc_recv, fw_send, fw_recv,
):
    n_chunk, n_x = whi.shape[0], whi.shape[1]
    boxes, comps, q = pat.shape
    group = cos.shape[0]
    s_count = boxes // group
    rows = s_count * comps
    p_all = idx.shape[1]
    p_own = p_all // (n_x * 2)
    sub = p_own // n_chunk
    n = group * q
    c_reach = child_coef.shape[1] // 2
    reach = coef.shape[1] // 2
    me = lax.axis_index("dir")
    box = lax.axis_index("box")
    n_box = lax.axis_size("box")
    x, core = me // 2, me % 2
    mate = 2 * x + 1 - core
    across = 2 * (1 - x) + core
    has_low, has_high = box > 0, box < n_box - 1

    def remote(src, dst, send, recv, to):
        return pltpu.make_async_remote_copy(
            src_ref=src, dst_ref=dst, send_sem=send, recv_sem=recv, device_id=to, device_id_type=MESH
        )

    load = pltpu.make_async_copy(pat, cbuf.at[pl.ds(c_reach, boxes)], local_sem)
    load.start()

    barrier = pltpu.get_barrier_semaphore()
    pl.semaphore_signal(barrier, inc=1, device_id={"dir": mate}, device_id_type=MESH)
    pl.semaphore_signal(barrier, inc=1, device_id={"dir": across}, device_id_type=MESH)

    @pl.when(has_low)
    def _():
        pl.semaphore_signal(barrier, inc=1, device_id={"box": box - 1}, device_id_type=MESH)

    @pl.when(has_high)
    def _():
        pl.semaphore_signal(barrier, inc=1, device_id={"box": box + 1}, device_id_type=MESH)

    pl.semaphore_wait(barrier, 2 + has_low.astype(jnp.int32) + has_high.astype(jnp.int32))

    def child_down():
        return remote(cbuf.at[pl.ds(c_reach, c_reach)], cbuf.at[pl.ds(c_reach + boxes, c_reach)],
                      ch_send.at[0], ch_recv.at[0], {"box": box - 1})

    def child_up():
        return remote(cbuf.at[pl.ds(boxes, c_reach)], cbuf.at[pl.ds(0, c_reach)],
                      ch_send.at[1], ch_recv.at[1], {"box": box + 1})

    def core_copy(j, a):
        return remote(part.at[j, 2 * a + 1 - core], crecv.at[j, a],
                      core_send.at[j, a], core_recv.at[j, a], {"dir": mate})

    def x_copy(j):
        return remote(xsend.at[j], xrecv.at[j], x_send.at[j], x_recv.at[j], {"dir": across})

    def halo_down(j):
        return remote(field.at[j, pl.ds(reach, reach)], field.at[j, pl.ds(reach + s_count, reach)],
                      halo_send.at[j, 0], halo_recv.at[j, 0], {"box": box - 1})

    def halo_up(j):
        return remote(field.at[j, pl.ds(s_count, reach)], field.at[j, pl.ds(0, reach)],
                      halo_send.at[j, 1], halo_recv.at[j, 1], {"box": box + 1})

    def local_x(j):
        return remote(gl.at[j, me], gl.at[j, me], lx_send.at[j], lx_recv.at[j], {"dir": across})

    def local_core(j):
        return remote(gl.at[j, me], gl.at[j, me], lc_send.at[j], lc_recv.at[j], {"dir": mate})

    def forward(j):
        return remote(gl.at[j, across], gl.at[j, across], fw_send.at[j], fw_recv.at[j], {"dir": mate})

    load.wait()

    @pl.when(has_low)
    def _():
        child_down().start()

    @pl.when(has_high)
    def _():
        child_up().start()

    for g in range(group):
        y = cbuf[c_reach : c_reach + boxes].reshape(s_count, group, comps, q)[:, g]
        for part_no, z in enumerate((y, turn(y))):
            hi, lo = split(z.reshape(rows, q))
            at = (part_no * group + g) * q
            xhi[:, at : at + q] = hi
            xlo[:, at : at + q] = lo

    first = me * q

    def send_x(j):
        for a in range(n_x):
            core_copy(j, a).wait_recv()
        xsend[j] = part[j, across] + crecv[j, 1 - x]
        x_copy(j).start()

    def upward(j, _):
        def half(a, _):
            for c in range(2):
                cols = pl.ds(pl.multiple_of((2 * a + c) * p_own + j * sub, sub), sub)
                row_no = first + lax.broadcasted_iota(jnp.int32, (q, sub), 0)
                m = jnp.zeros((q, sub), F32)
                for k in range(idx.shape[0]):
                    m = m + jnp.where(row_no == idx[k : k + 1, cols], wgt[k : k + 1, cols], F32(0.0))
                for part_no, table in enumerate((cos, sin)):
                    for g in range(group):
                        hi, lo = split(m * table[g : g + 1, cols])
                        at = (part_no * group + g) * q
                        whi[j, a, at : at + q, c * sub : (c + 1) * sub] = hi
                        wlo[j, a, at : at + q, c * sub : (c + 1) * sub] = lo
            total = nn(xhi[...], whi[j, a]) + nn(xhi[...], wlo[j, a]) + nn(xlo[...], whi[j, a])
            for c in range(2):
                part[j, 2 * a + c] = total[:, c * sub : (c + 1) * sub].reshape(s_count, comps, sub)
            core_copy(j, a).start()
            return 0

        lax.fori_loop(0, n_x, half, 0)

        @pl.when(j > 0)
        def _():
            send_x(j - 1)

        return 0

    lax.fori_loop(0, n_chunk, upward, 0)
    send_x(n_chunk - 1)

    @pl.when(jnp.logical_not(has_low))
    def _():
        cbuf[0:c_reach] = jnp.zeros((c_reach, comps, q), F32)
        for j in range(n_chunk):
            field[j, 0:reach] = jnp.zeros((reach, comps, sub), F32)

    @pl.when(jnp.logical_not(has_high))
    def _():
        cbuf[c_reach + boxes :] = jnp.zeros((c_reach, comps, q), F32)
        for j in range(n_chunk):
            field[j, reach + s_count :] = jnp.zeros((reach, comps, sub), F32)

    @pl.when(has_low)
    def _():
        child_up().wait_recv()

    @pl.when(has_high)
    def _():
        child_down().wait_recv()

    quarter = boxes // n_chunk

    def middle(j, _):
        @pl.when(j < n_chunk)
        def _():
            x_copy(j).wait_recv()
            field[j, reach : reach + s_count] = part[j, me] + crecv[j, x] + xrecv[j]

            @pl.when(has_low)
            def _():
                halo_down(j).start()

            @pl.when(has_high)
            def _():
                halo_up(j).start()

            def put(s, v):
                out[s] = v

            translate(
                lambda i: cbuf[i], c_reach, lambda r, k: child_coef[r, k : k + 1, :],
                lambda k, s: child_mask[k, s], put, j * quarter, quarter, c_reach,
            )

        @pl.when(j > 0)
        def _():
            i = j - 1

            @pl.when(has_low)
            def _():
                halo_up(i).wait_recv()

            @pl.when(has_high)
            def _():
                halo_down(i).wait_recv()

            def put(s, v):
                gl[i, me, s] = v

            cols = pl.ds(pl.multiple_of(i * sub, sub), sub)
            translate(
                lambda s: field[i, s], reach, lambda r, k: coef[r, k : k + 1, cols],
                lambda k, s: mask[k, s], put, 0, s_count, reach,
            )
            local_x(i).start()
            local_core(i).start()

        @pl.when(j > 1)
        def _():
            local_x(j - 2).wait_recv()
            forward(j - 2).start()

        return 0

    lax.fori_loop(0, n_chunk + 1, middle, 0)

    def downward(j, _):
        @pl.when(j == 1)
        def _():
            local_x(n_chunk - 1).wait_recv()
            forward(n_chunk - 1).start()

        local_core(j).wait_recv()
        forward(j).wait_recv()
        total = None
        for a in range(n_x):
            y = [gl[j, 2 * a + c] for c in range(2)]
            for part_no in range(2):
                z = y if part_no == 0 else [-turn(v) for v in y]
                hi, lo = split(jnp.concatenate([v.reshape(rows, sub) for v in z], axis=1))
                wh = whi[j, a, part_no * n : (part_no + 1) * n, :]
                wl = wlo[j, a, part_no * n : (part_no + 1) * n, :]
                for term in (nt(hi, wh), nt(hi, wl), nt(lo, wh)):
                    total = term if total is None else total + term

        @pl.when(j == 0)
        def _():
            acc[...] = total

        @pl.when(j > 0)
        def _():
            acc[...] = acc[...] + total

        return 0

    lax.fori_loop(0, n_chunk, downward, 0)

    def put_out(s, _):
        at = pl.ds(pl.multiple_of(s * comps, comps), comps)
        for g in range(group):
            out[s * group + g] = out[s * group + g] + acc[at, g * q : (g + 1) * q]
        return 0

    lax.fori_loop(0, s_count, put_out, 0)

    def finish(j, _):
        for a in range(n_x):
            core_copy(j, a).wait_send()
        x_copy(j).wait_send()
        local_x(j).wait_send()
        local_core(j).wait_send()
        forward(j).wait_send()

        @pl.when(has_low)
        def _():
            halo_down(j).wait_send()

        @pl.when(has_high)
        def _():
            halo_up(j).wait_send()

        return 0

    lax.fori_loop(0, n_chunk, finish, 0)

    @pl.when(has_low)
    def _():
        child_down().wait_send()

    @pl.when(has_high)
    def _():
        child_up().wait_send()


def body(pattern, child_coef, child_mask, interp_index, interp_weight, phase_angle, parent_coef, parent_mask):
    q, comps, boxes = pattern.shape
    p_all = interp_index.shape[1]
    group = phase_angle.shape[0]
    s_count = boxes // group
    n_x = lax.axis_size("dir") // 2
    p_own = p_all // (2 * n_x)
    sub = 128
    n_chunk = p_own // sub
    rows, wsize = s_count * comps, 2 * group * q
    c_reach = child_coef.shape[1] // 2
    reach = parent_coef.shape[1] // 2
    dir_rank = lax.axis_index("dir")
    box_rank = lax.axis_index("box")
    cos, sin = jnp.cos(phase_angle), jnp.sin(phase_angle)
    pat = jnp.transpose(pattern, (2, 1, 0))
    own_coef = lax.dynamic_slice_in_dim(parent_coef, dir_rank * p_own, p_own, 2)
    own_mask = lax.dynamic_slice_in_dim(parent_mask, box_rank * s_count, s_count, 1).astype(F32)
    vmem = pl.BlockSpec(memory_space=pltpu.VMEM)
    smem = pl.BlockSpec(memory_space=pltpu.SMEM)
    dma = pltpu.SemaphoreType.DMA
    block = (s_count, comps, sub)
    out = pl.pallas_call(
        kernel,
        out_shape=jax.ShapeDtypeStruct((boxes, comps, q), F32),
        in_specs=[vmem] * 6 + [smem] * 2 + [pl.BlockSpec(memory_space=pl.ANY)],
        out_specs=vmem,
        scratch_shapes=[
            pltpu.VMEM((boxes + 2 * c_reach, comps, q), F32),
            pltpu.VMEM((rows, wsize), BF16),
            pltpu.VMEM((rows, wsize), BF16),
            pltpu.VMEM((n_chunk, n_x, wsize, 2 * sub), BF16),
            pltpu.VMEM((n_chunk, n_x, wsize, 2 * sub), BF16),
            pltpu.VMEM((n_chunk, 2 * n_x) + block, F32),
            pltpu.VMEM((n_chunk, n_x) + block, F32),
            pltpu.VMEM((n_chunk,) + block, F32),
            pltpu.VMEM((n_chunk,) + block, F32),
            pltpu.VMEM((n_chunk, s_count + 2 * reach, comps, sub), F32),
            pltpu.VMEM((n_chunk, 2 * n_x) + block, F32),
            pltpu.VMEM((rows, group * q), F32),
            dma(()), dma((2,)), dma((2,)),
            dma((n_chunk, n_x)), dma((n_chunk, n_x)),
            dma((n_chunk,)), dma((n_chunk,)),
            dma((n_chunk, 2)), dma((n_chunk, 2)),
        ] + [dma((n_chunk,))] * 6,
        compiler_params=pltpu.CompilerParams(
            vmem_limit_bytes=VMEM_LIMIT, collective_id=0, has_side_effects=True
        ),
    )(interp_index, interp_weight, cos, sin, child_coef, own_coef, child_mask.astype(F32), own_mask, pat)
    return jnp.transpose(out, (2, 1, 0))


def solution(mesh):
    placed = (P("dir", None, "box"), P(None, None, "dir"), P(None, "box"), P(), P(), P(), P(), P())
    return jax.shard_map(
        body, mesh=mesh, in_specs=placed, out_specs=P("dir", None, "box"), check_vma=False
    )
```
